32 devices in a mesh: tower: 2 (over x), member: 16 (over z, y, core).
Axes of the slice: x: 2, y: 2, z: 4, core: 2. Of those that a mesh axis runs over, the one named last changes fastest.
Arguments:
- features: bfloat16 [4, 8192, 64], P('tower', 'member'), may hold values from -6 to 6
- compress: bfloat16 [4, 8192, 256], P('tower', 'member'), may hold values from -0.0625 to 0.0625
- top_down: bfloat16 [1024, 256], replicated, may hold values from -0.1875 to 0.1875
- top_up: bfloat16 [1024, 256], replicated, may hold values from -0.375 to 0.375
- top_bias: float32 [1024], replicated, may hold values from -3 to 3
- out_weight: bfloat16 [1024], replicated, may hold values from -0.1875 to 0.1875
- labels: int32 [64], replicated, may hold values 0 or 1
Outputs:
- grad_compress: float32 [4, 8192, 256], P('tower', 'member')
- grad_features: bfloat16 [4, 8192, 64], P('tower', 'member')
- grad_down: float32 [1024, 256], P(('tower', 'member'))
- grad_up: float32 [1024, 256], P(('tower', 'member'))
- grad_vectors: float32 [2, 1024], P(None, ('tower', 'member'))
The draws below stay inside these ranges and needn't reach their ends.
All inputs are finite; a program needn't handle non-finite values.
Results may differ from the reference program's by a relative error of at most 0.0075.
Values may be sent and summed in bfloat16 or wider, within the bound.
No kernel may reach another device: no remote copies, remote signals or barrier semaphores. Data moves between devices by JAX's collectives and lax.ppermute only.
A program may use at most 64 MiB of HBM per device.

```python
import jax
import jax.numpy as jnp
from jax import lax

TW = 8192
COMP = 256
RANK = 256
TOWERS = 4
BATCH = 64
TOP = 1024


def with_ends(values, stream_key, low, top_value):
    extent = values.shape
    spot = [jax.random.randint(jax.random.fold_in(stream_key, axis), (), 0, extent[axis]) for axis in range(len(extent))]
    values = values.at[tuple(spot)].set(low)
    longest = extent.index(max(extent))
    spot[longest] = (spot[longest] + 1) % extent[longest]
    return values.at[tuple(spot)].set(top_value)


def shard_levels(stream_key, extent, cuts, least, largest):
    loudness, own = 1.0, jax.random.fold_in(stream_key, 6)
    for dim, blocks in cuts:
        heights = jnp.exp(jax.random.uniform(jax.random.fold_in(own, dim), (blocks,), jnp.float32, least / len(cuts), largest / len(cuts)))
        loudness = loudness * jnp.repeat(heights, extent[dim] // blocks).reshape([-1 if axis == dim else 1 for axis in range(len(extent))])
    return loudness


def gaussian(rng, extent, deviation, reach, cuts=(), kind=jnp.bfloat16):
    drawn = deviation * jax.random.normal(rng, extent, jnp.float32)
    if cuts:
        drawn = drawn * shard_levels(rng, extent, cuts, -0.22, 0.18)
    return jnp.clip(drawn, -reach, reach).astype(kind)


def setup_inputs(seed: int = 0) -> dict:
    keys = jax.random.split(jax.random.key(seed), 8)
    features = gaussian(keys[0], (TOWERS, TW, BATCH), 1.0, 6.0, ((0, 2), (1, 16)))
    compress = gaussian(keys[1], (TOWERS, TW, COMP), TW ** -0.5, 0.0625, ((0, 2), (1, 16)))
    top_down = gaussian(keys[2], (TOP, RANK), TOP ** -0.5, 0.1875)
    top_up = gaussian(keys[3], (TOP, RANK), RANK ** -0.5, 0.375)
    top_bias = gaussian(keys[4], (TOP,), 0.5, 3.0, (), jnp.float32)
    out_weight = gaussian(keys[5], (TOP,), TOP ** -0.5, 0.1875)
    labels = with_ends((jax.random.randint(keys[6], (BATCH,), 0, 2) < 1).astype(jnp.int32), jax.random.fold_in(keys[6], 1), 0, 1)
    return {"features": features, "compress": compress, "top_down": top_down, "top_up": top_up, "top_bias": top_bias, "out_weight": out_weight, "labels": labels}


def contract_rows(left, right):
    return lax.dot_general(left, right, (((0,), (0,)), ((), ())), preferred_element_type=jnp.float32)


def reference(features, compress, top_down, top_up, top_bias, out_weight, labels):
    stacked = lax.map(lambda pair: contract_rows(pair[0], pair[1]), (features, compress))
    compressed = jnp.transpose(stacked, (1, 0, 2)).reshape(BATCH, TOP).astype(jnp.bfloat16)
    lowrank = jnp.dot(compressed, top_down, preferred_element_type=jnp.float32).astype(jnp.bfloat16)
    gate = lax.dot_general(lowrank, top_up, (((1,), (1,)), ((), ())), preferred_element_type=jnp.float32) + top_bias
    comp_f = compressed.astype(jnp.float32)
    crossed = comp_f * gate + comp_f
    wout = out_weight.astype(jnp.float32)
    logit = jnp.sum(crossed * wout[None, :], axis=1)
    dlogit = jax.nn.sigmoid(logit) - labels.astype(jnp.float32)
    dcrossed = dlogit[:, None] * wout[None, :]
    dgate_f = dcrossed * comp_f
    grad_vectors = jnp.stack([jnp.sum(dgate_f, axis=0), jnp.sum(dlogit[:, None] * crossed, axis=0)])
    dgate = dgate_f.astype(jnp.bfloat16)
    grad_up = contract_rows(dgate, lowrank)
    dlowrank = jnp.dot(dgate, top_up, preferred_element_type=jnp.float32).astype(jnp.bfloat16)
    grad_down = contract_rows(compressed, dlowrank)
    dcomp = dcrossed * (gate + 1.0) + lax.dot_general(dlowrank, top_down, (((1,), (1,)), ((), ())), preferred_element_type=jnp.float32)
    dcomp = dcomp.astype(jnp.bfloat16)
    dslices = jnp.transpose(dcomp.reshape(BATCH, TOWERS, COMP), (1, 0, 2))

    def per_tower(triple):
        feat, weight, cot = triple
        grad_w = jnp.dot(feat, cot, preferred_element_type=jnp.float32)
        grad_x = lax.dot_general(weight, cot, (((1,), (1,)), ((), ())), preferred_element_type=jnp.float32)
        return grad_w, grad_x.astype(jnp.bfloat16)

    grad_w, grad_x = lax.map(per_tower, (features, compress, dslices))
    return (grad_w, grad_x, grad_down, grad_up, grad_vectors)
```

```python
import jax
import jax.numpy as jnp
from jax import lax
from jax.sharding import PartitionSpec as P


def contract_rows(left, right):
    return lax.dot_general(
        left, right, (((0,), (0,)), ((), ())), preferred_element_type=jnp.float32
    )


def cross_top(compressed, down, upper, bias, wout, target, sum_low, sum_score, sum_back):
    lowrank = sum_low(jnp.dot(compressed, down, preferred_element_type=jnp.float32)).astype(
        jnp.bfloat16
    )
    gate = (
        lax.dot_general(
            lowrank, upper, (((1,), (1,)), ((), ())), preferred_element_type=jnp.float32
        )
        + bias
    )
    comp_f = compressed.astype(jnp.float32)
    crossed = comp_f * gate + comp_f
    wide_out = wout.astype(jnp.float32)
    logit = sum_score(jnp.sum(crossed * wide_out[None, :], axis=1))
    dlogit = jax.nn.sigmoid(logit) - target
    dcrossed = dlogit[:, None] * wide_out[None, :]
    dgate_f = dcrossed * comp_f
    vectors = jnp.stack([jnp.sum(dgate_f, axis=0), jnp.sum(dlogit[:, None] * crossed, axis=0)])
    dgate = dgate_f.astype(jnp.bfloat16)
    grad_up = contract_rows(dgate, lowrank)
    dlowrank = sum_back(jnp.dot(dgate, upper, preferred_element_type=jnp.float32)).astype(
        jnp.bfloat16
    )
    grad_down = contract_rows(compressed, dlowrank)
    dcomp = dcrossed * (gate + 1.0) + lax.dot_general(
        dlowrank, down, (((1,), (1,)), ((), ())), preferred_element_type=jnp.float32
    )
    return (dcomp.astype(jnp.bfloat16), grad_down, grad_up, vectors)


def shards_spread(features, compress, top_down, top_up, top_bias, out_weight, labels):
    local_towers, feat_rows, batch = features.shape
    comp_width = compress.shape[2]
    group_width = local_towers * comp_width
    mine = batch // lax.axis_size("member")
    member_idx = lax.axis_index("member")
    tower_idx = lax.axis_index("tower")
    block = features
    term = jnp.einsum("kfn,kfc->nkc", block, compress, preferred_element_type=jnp.float32)
    local = lax.psum_scatter(
        term.reshape(mine * lax.axis_size("member"), group_width),
        "member",
        scatter_dimension=0,
        tiled=True,
    ).astype(jnp.bfloat16)
    offset = tower_idx * group_width
    down_t = lax.dynamic_slice_in_dim(top_down, offset, group_width, 0)
    upper_t = lax.dynamic_slice_in_dim(top_up, offset, group_width, 0)
    bias_t = lax.dynamic_slice_in_dim(top_bias, offset, group_width, 0)
    wout_t = lax.dynamic_slice_in_dim(out_weight, offset, group_width, 0)
    target = lax.dynamic_slice_in_dim(labels, member_idx * mine, mine, 0).astype(jnp.float32)
    dcomp, grad_down, grad_up, vectors = cross_top(
        local,
        down_t,
        upper_t,
        bias_t,
        wout_t,
        target,
        lambda value: lax.psum(value, "tower"),
        lambda value: lax.psum(value, "tower"),
        lambda value: lax.psum(value, "tower"),
    )
    grad_down, grad_up, vectors = (
        lax.psum_scatter(grad_down, "member", scatter_dimension=0, tiled=True),
        lax.psum_scatter(grad_up, "member", scatter_dimension=0, tiled=True),
        lax.psum_scatter(vectors, "member", scatter_dimension=1, tiled=True),
    )
    piece = lax.all_gather(dcomp, "member", axis=0, tiled=True)
    count = piece.shape[0]
    block = features
    split_piece = piece.reshape(count, local_towers, comp_width)
    grad_w = jnp.einsum("kfn,nkc->kfc", block, split_piece, preferred_element_type=jnp.float32)
    column = jnp.einsum("kfc,nkc->kfn", compress, split_piece, preferred_element_type=jnp.float32)
    grad_x = column
    grad_w, grad_x = (grad_w, grad_x)
    return (grad_w, grad_x.astype(jnp.bfloat16), grad_down, grad_up, vectors)


def nt(left, right):
    return lax.dot_general(
        left, right, (((1,), (1,)), ((), ())), preferred_element_type=jnp.float32
    )


def exchange(value, tower_bit, member_bit):
    towers, members = lax.axis_size("tower"), lax.axis_size("member")
    pairs = [
        (t * members + m, (t ^ tower_bit) * members + (m ^ member_bit))
        for t in range(towers)
        for m in range(members)
    ]
    return lax.ppermute(value, ("tower", "member"), pairs)


def shards_doubling(features, compress, top_down, top_up, top_bias, out_weight, labels):
    local_towers, feat_rows, batch = features.shape
    comp_width = compress.shape[2]
    members = lax.axis_size("member")
    half = local_towers // 2
    member_idx = lax.axis_index("member")
    tower_idx = lax.axis_index("tower")
    side = member_idx % 2
    term = jnp.einsum("kfn,kfc->knc", features, compress, preferred_element_type=jnp.float32)
    kept = lax.dynamic_slice_in_dim(term, side * half, half, 0)
    sent = lax.dynamic_slice_in_dim(term, (1 - side) * half, half, 0)
    total = kept + exchange(sent, 0, 1)
    stride = 2
    while stride < members:
        total = total + exchange(total, 0, stride)
        stride *= 2
    mine = total.astype(jnp.bfloat16)
    pieces = {
        (t, s): mine if (t, s) == (0, 0) else exchange(mine, t, s) for t in (0, 1) for s in (0, 1)
    }
    by_side = []
    for t in (0, 1):
        near, far = pieces[t, 0], pieces[t, 1]
        by_side.append(
            jnp.concatenate([jnp.where(side == 0, near, far), jnp.where(side == 0, far, near)], 0)
        )
    parts = jnp.concatenate(
        [
            jnp.where(tower_idx == 0, by_side[0], by_side[1]),
            jnp.where(tower_idx == 0, by_side[1], by_side[0]),
        ],
        0,
    )
    compressed = jnp.transpose(parts, (1, 0, 2)).reshape(batch, -1)
    lowrank = jnp.dot(compressed, top_down, preferred_element_type=jnp.float32).astype(jnp.bfloat16)
    gate = nt(lowrank, top_up) + top_bias
    comp_f = compressed.astype(jnp.float32)
    crossed = comp_f * gate + comp_f
    wide_out = out_weight.astype(jnp.float32)
    logit = jnp.sum(crossed * wide_out[None, :], axis=1)
    dlogit = jax.nn.sigmoid(logit) - labels.astype(jnp.float32)
    dcrossed = dlogit[:, None] * wide_out[None, :]
    dgate_f = dcrossed * comp_f
    vectors = jnp.stack([jnp.sum(dgate_f, axis=0), jnp.sum(dlogit[:, None] * crossed, axis=0)])
    dgate = dgate_f.astype(jnp.bfloat16)
    dlowrank = jnp.dot(dgate, top_up, preferred_element_type=jnp.float32).astype(jnp.bfloat16)
    width = compressed.shape[1] // (2 * members)
    column = (tower_idx * members + member_idx) * width
    own = lambda value: lax.dynamic_slice_in_dim(value, column, width, 1)
    grad_up = contract_rows(own(dgate), lowrank)
    grad_down = contract_rows(own(compressed), dlowrank)
    group = local_towers * comp_width
    block = lambda value, dim: lax.dynamic_slice_in_dim(value, tower_idx * group, group, dim)
    dcomp = (
        block(dcrossed, 1) * (block(gate, 1) + 1.0) + nt(dlowrank, block(top_down, 0))
    ).astype(jnp.bfloat16)
    dparts = dcomp.reshape(batch, local_towers, comp_width)
    grad_w = jnp.einsum("kfn,nkc->kfc", features, dparts, preferred_element_type=jnp.float32)
    grad_x = jnp.einsum("kfc,nkc->kfn", compress, dparts, preferred_element_type=jnp.float32)
    return (grad_w, grad_x.astype(jnp.bfloat16), grad_down, grad_up, own(vectors))


def solution(mesh):
    members = mesh.shape["member"]
    small = mesh.shape["tower"] == 2 and members >= 2 and members & (members - 1) == 0
    shards = shards_doubling if small else shards_spread
    placed = (P("tower", "member", None), P("tower", "member", None), P(), P(), P(), P(), P())
    return jax.shard_map(
        shards,
        mesh=mesh,
        in_specs=placed,
        out_specs=(
            P("tower", "member", None),
            P("tower", "member", None),
            P(("tower", "member"), None),
            P(("tower", "member"), None),
            P(None, ("tower", "member")),
        ),
        check_vma=False,
    )
```

```python
import functools

import jax
import jax.numpy as jnp
from jax import lax
from jax.experimental import pallas as pl
from jax.experimental.pallas import tpu as pltpu
from jax.sharding import PartitionSpec as P


def contract_rows(left, right):
    return lax.dot_general(
        left, right, (((0,), (0,)), ((), ())), preferred_element_type=jnp.float32
    )


def cross_top(compressed, down, upper, bias, wout, target, sum_low, sum_score, sum_back):
    lowrank = sum_low(jnp.dot(compressed, down, preferred_element_type=jnp.float32)).astype(
        jnp.bfloat16
    )
    gate = (
        lax.dot_general(
            lowrank, upper, (((1,), (1,)), ((), ())), preferred_element_type=jnp.float32
        )
        + bias
    )
    comp_f = compressed.astype(jnp.float32)
    crossed = comp_f * gate + comp_f
    wide_out = wout.astype(jnp.float32)
    logit = sum_score(jnp.sum(crossed * wide_out[None, :], axis=1))
    dlogit = jax.nn.sigmoid(logit) - target
    dcrossed = dlogit[:, None] * wide_out[None, :]
    dgate_f = dcrossed * comp_f
    vectors = jnp.stack([jnp.sum(dgate_f, axis=0), jnp.sum(dlogit[:, None] * crossed, axis=0)])
    dgate = dgate_f.astype(jnp.bfloat16)
    grad_up = contract_rows(dgate, lowrank)
    dlowrank = sum_back(jnp.dot(dgate, upper, preferred_element_type=jnp.float32)).astype(
        jnp.bfloat16
    )
    grad_down = contract_rows(compressed, dlowrank)
    dcomp = dcrossed * (gate + 1.0) + lax.dot_general(
        dlowrank, down, (((1,), (1,)), ((), ())), preferred_element_type=jnp.float32
    )
    return (dcomp.astype(jnp.bfloat16), grad_down, grad_up, vectors)


def shards_spread(features, compress, top_down, top_up, top_bias, out_weight, labels):
    local_towers, feat_rows, batch = features.shape
    comp_width = compress.shape[2]
    group_width = local_towers * comp_width
    mine = batch // lax.axis_size("member")
    member_idx = lax.axis_index("member")
    tower_idx = lax.axis_index("tower")
    block = features
    term = jnp.einsum("kfn,kfc->nkc", block, compress, preferred_element_type=jnp.float32)
    local = lax.psum_scatter(
        term.reshape(mine * lax.axis_size("member"), group_width),
        "member",
        scatter_dimension=0,
        tiled=True,
    ).astype(jnp.bfloat16)
    offset = tower_idx * group_width
    down_t = lax.dynamic_slice_in_dim(top_down, offset, group_width, 0)
    upper_t = lax.dynamic_slice_in_dim(top_up, offset, group_width, 0)
    bias_t = lax.dynamic_slice_in_dim(top_bias, offset, group_width, 0)
    wout_t = lax.dynamic_slice_in_dim(out_weight, offset, group_width, 0)
    target = lax.dynamic_slice_in_dim(labels, member_idx * mine, mine, 0).astype(jnp.float32)
    dcomp, grad_down, grad_up, vectors = cross_top(
        local,
        down_t,
        upper_t,
        bias_t,
        wout_t,
        target,
        lambda value: lax.psum(value, "tower"),
        lambda value: lax.psum(value, "tower"),
        lambda value: lax.psum(value, "tower"),
    )
    grad_down, grad_up, vectors = (
        lax.psum_scatter(grad_down, "member", scatter_dimension=0, tiled=True),
        lax.psum_scatter(grad_up, "member", scatter_dimension=0, tiled=True),
        lax.psum_scatter(vectors, "member", scatter_dimension=1, tiled=True),
    )
    piece = lax.all_gather(dcomp, "member", axis=0, tiled=True)
    count = piece.shape[0]
    block = features
    split_piece = piece.reshape(count, local_towers, comp_width)
    grad_w = jnp.einsum("kfn,nkc->kfc", block, split_piece, preferred_element_type=jnp.float32)
    column = jnp.einsum("kfc,nkc->kfn", compress, split_piece, preferred_element_type=jnp.float32)
    grad_x = column
    grad_w, grad_x = (grad_w, grad_x)
    return (grad_w, grad_x.astype(jnp.bfloat16), grad_down, grad_up, vectors)


F32, BF16 = jnp.float32, jnp.bfloat16
VMEM = pl.BlockSpec(memory_space=pltpu.VMEM)
ANY = pl.BlockSpec(memory_space=pl.ANY)
CHUNKS = 4


def nt(left, right):
    return lax.dot_general(left, right, (((1,), (1,)), ((), ())), preferred_element_type=F32)


def exchange(value, tower_bit, member_bit):
    towers, members = lax.axis_size("tower"), lax.axis_size("member")
    pairs = [
        (t * members + m, (t ^ tower_bit) * members + (m ^ member_bit))
        for t in range(towers)
        for m in range(members)
    ]
    return lax.ppermute(value, ("tower", "member"), pairs)


def term_kernel(flip, feat_hbm, comp_hbm, out, feat, comp, sems):
    which = lax.rem(lax.axis_index("member") + flip, 2)
    rows = comp.shape[1]
    load_feat = pltpu.make_async_copy(feat_hbm.at[which], feat, sems.at[2])
    loads = [
        pltpu.make_async_copy(
            comp_hbm.at[which, pl.ds(i * rows, rows)], comp.at[i], sems.at[i]
        )
        for i in range(2)
    ]
    load_feat.start()
    for load in loads:
        load.start()
    load_feat.wait()
    total = None
    for i in range(2):
        loads[i].wait()
        part = jnp.dot(feat[:, i * rows : (i + 1) * rows], comp[i], preferred_element_type=F32)
        total = part if total is None else total + part
    out[...] = total


def term(flip, feat_t, compress):
    _, batch, rows = feat_t.shape
    width = compress.shape[2]
    return pl.pallas_call(
        lambda *refs: term_kernel(flip, *refs),
        out_shape=jax.ShapeDtypeStruct((batch, width), F32),
        in_specs=[ANY, ANY],
        out_specs=VMEM,
        scratch_shapes=[
            pltpu.VMEM((batch, rows), BF16),
            pltpu.VMEM((2, rows // 2, width), BF16),
            pltpu.SemaphoreType.DMA((3,)),
        ],
        compiler_params=pltpu.CompilerParams(vmem_limit_bytes=2 << 20),
        cost_estimate=pl.CostEstimate(
            flops=2 * batch * rows * width, bytes_accessed=2 * rows * (width + batch), transcendentals=0
        ),
    )(
        pltpu.with_memory_space_constraint(feat_t, pltpu.HBM),
        pltpu.with_memory_space_constraint(compress, pltpu.HBM),
    )


def top_kernel(
    mine, side_piece, tower_piece, both_piece, down, upper, bias, wout, labels_hbm, feat, comp,
    grad_w_hbm, grad_x, grad_down, grad_up, vectors,
    compressed, gates, wide, labels, grad_w, square, sems,
):
    tower, member = lax.axis_index("tower"), lax.axis_index("member")
    side = lax.rem(member, 2)
    batch, width = mine.shape
    pieces = compressed.shape[0]
    load_labels = pltpu.make_async_copy(labels_hbm, labels, sems.at[CHUNKS])
    load_labels.start()
    compressed[2 * tower + side] = mine[...]
    compressed[2 * tower + 1 - side] = side_piece[...]
    compressed[2 * (1 - tower) + side] = tower_piece[...]
    compressed[2 * (1 - tower) + 1 - side] = both_piece[...]
    block = lambda j: slice(j * width, (j + 1) * width)
    summed = lambda parts: functools.reduce(jnp.add, parts)

    low = summed(
        jnp.dot(compressed[j], down[block(j), :], preferred_element_type=F32)
        for j in range(pieces)
    ).astype(BF16)
    weighted, scores = [], []
    for j in range(pieces):
        gate = nt(low, upper[block(j), :]) + bias[:, block(j)]
        gates[j] = gate
        out_row = wout[:, block(j)].astype(F32)
        wide[j] = out_row
        comp_f = compressed[j].astype(F32)
        weighted.append((comp_f * out_row).astype(BF16))
        scores.append((comp_f * gate + comp_f) * out_row)
    logit = jnp.sum(summed(scores), axis=1, keepdims=True)
    back = summed(
        jnp.dot(weighted[j], upper[block(j), :], preferred_element_type=F32)
        for j in range(pieces)
    )
    back_low = back.astype(BF16)
    slopes = []
    for k in range(2):
        j = 2 * tower + k
        rows = pl.ds(pl.multiple_of(j * width, width), width)
        slopes.append(wide[j] * (gates[j] + 1.0) + nt(back_low, down[rows, :]))
    row = lax.broadcasted_iota(jnp.int32, (batch, batch), 0)
    col = lax.broadcasted_iota(jnp.int32, (batch, batch), 1)
    load_labels.wait()
    target = jnp.sum(jnp.where(row == col, labels[...].astype(F32), 0.0), axis=1, keepdims=True)
    dlogit = 1.0 / (1.0 + jnp.exp(-logit)) - target

    stores = []
    size = grad_w.shape[1]
    per_tower = CHUNKS // 2
    dcomps = [(dlogit * slope).astype(BF16) for slope in slopes]
    for i in range(CHUNKS):
        k, part = i // per_tower, i % per_tower
        grad_w[i] = contract_rows(feat[k, :, part * size : (part + 1) * size], dcomps[k])
        store = pltpu.make_async_copy(
            grad_w.at[i], grad_w_hbm.at[k, pl.ds(part * size, size)], sems.at[i]
        )
        store.start()
        stores.append(store)
    for k in range(2):
        grad_x[k] = nt(dcomps[k], comp[k]).astype(BF16)

    count = grad_down.shape[0]
    first = (tower * lax.axis_size("member") + member) * count
    own = lax.div(first, width)
    offset = pl.multiple_of(lax.rem(first, width), count)
    comp_f = compressed[own].astype(F32)
    dgate_f = dlogit * wide[own] * comp_f
    crossed = comp_f * gates[own] + comp_f
    square[...] = contract_rows(dgate_f.astype(BF16), low)
    grad_up[...] = square[pl.ds(offset, count), :]
    square[...] = contract_rows(compressed[own], (dlogit * back).astype(BF16))
    grad_down[...] = square[pl.ds(offset, count), :]
    sums = jnp.concatenate(
        [
            jnp.sum(dgate_f, axis=0, keepdims=True),
            jnp.sum(dlogit * crossed, axis=0, keepdims=True),
            jnp.zeros((6, width), F32),
        ],
        axis=0,
    )
    vectors[...] = pltpu.roll(sums, width - offset, 1)[0:2, 0:count]
    for store in stores:
        store.wait()


def shards_doubling(features, compress, top_down, top_up, top_bias, out_weight, labels):
    local_towers, feat_rows, batch = features.shape
    width = compress.shape[2]
    rank = top_down.shape[1]
    members = lax.axis_size("member")
    top = top_down.shape[0]
    count = top // (2 * members)
    pieces = top // width
    feat_t = jnp.swapaxes(features, 1, 2)
    total = term(0, feat_t, compress) + exchange(term(1, feat_t, compress), 0, 1)
    strides = [1 << bit for bit in range(1, members.bit_length() - 1)]
    if len(strides) > 1:
        one, two = strides.pop(0), strides.pop(0)
        total = total + sum(exchange(total, 0, bits) for bits in (one, two, one | two))
    for stride in strides:
        total = total + exchange(total, 0, stride)
    mine = total.astype(BF16)
    near = lambda value: pltpu.with_memory_space_constraint(value, pltpu.VMEM)
    grad_w, grad_x, grad_down, grad_up, vectors = pl.pallas_call(
        top_kernel,
        out_shape=(
            jax.ShapeDtypeStruct((local_towers, feat_rows, width), F32),
            jax.ShapeDtypeStruct((local_towers, batch, feat_rows), BF16),
            jax.ShapeDtypeStruct((count, rank), F32),
            jax.ShapeDtypeStruct((count, rank), F32),
            jax.ShapeDtypeStruct((2, count), F32),
        ),
        in_specs=[VMEM] * 8 + [ANY, VMEM, VMEM],
        out_specs=(ANY, VMEM, VMEM, VMEM, VMEM),
        scratch_shapes=[
            pltpu.VMEM((pieces, batch, width), BF16),
            pltpu.VMEM((pieces, batch, width), F32),
            pltpu.VMEM((pieces, 1, width), F32),
            pltpu.VMEM((1, batch), labels.dtype),
            pltpu.VMEM((CHUNKS, local_towers * feat_rows // CHUNKS, width), F32),
            pltpu.VMEM((width, rank), F32),
            pltpu.SemaphoreType.DMA((CHUNKS + 1,)),
        ],
        compiler_params=pltpu.CompilerParams(vmem_limit_bytes=8 << 20),
        cost_estimate=pl.CostEstimate(
            flops=10 * batch * top * rank, bytes_accessed=4 << 20, transcendentals=batch
        ),
    )(
        near(mine),
        near(exchange(mine, 0, 1)),
        near(exchange(mine, 1, 0)),
        near(exchange(mine, 1, 1)),
        near(top_down),
        near(top_up),
        near(top_bias.reshape(1, top)),
        near(out_weight.reshape(1, top)),
        pltpu.with_memory_space_constraint(labels.reshape(1, batch), pltpu.HBM),
        near(feat_t),
        near(compress),
    )
    return grad_w, jnp.swapaxes(grad_x, 1, 2), grad_down, grad_up, vectors


def shards(features, compress, top_down, *rest):
    towers, members = lax.axis_size("tower"), lax.axis_size("member")
    small = towers == 2 and features.shape[0] == 2 and features.shape[2] <= 128
    power = members > 1 and members & (members - 1) == 0
    body = shards_doubling if small and power else shards_spread
    return body(features, compress, top_down, *rest)


def solution(mesh):
    placed = (P("tower", "member", None), P("tower", "member", None), P(), P(), P(), P(), P())
    return jax.shard_map(
        shards,
        mesh=mesh,
        in_specs=placed,
        out_specs=(
            P("tower", "member", None),
            P("tower", "member", None),
            P(("tower", "member"), None),
            P(("tower", "member"), None),
            P(None, ("tower", "member")),
        ),
        check_vma=False,
    )
```

```python
import functools

import jax
import jax.numpy as jnp
from jax import lax
from jax.experimental import pallas as pl
from jax.experimental.pallas import tpu as pltpu
from jax.sharding import PartitionSpec as P


def contract_rows(left, right):
    return lax.dot_general(
        left, right, (((0,), (0,)), ((), ())), preferred_element_type=jnp.float32
    )


def cross_top(compressed, down, upper, bias, wout, target, sum_low, sum_score, sum_back):
    lowrank = sum_low(jnp.dot(compressed, down, preferred_element_type=jnp.float32)).astype(
        jnp.bfloat16
    )
    gate = (
        lax.dot_general(
            lowrank, upper, (((1,), (1,)), ((), ())), preferred_element_type=jnp.float32
        )
        + bias
    )
    comp_f = compressed.astype(jnp.float32)
    crossed = comp_f * gate + comp_f
    wide_out = wout.astype(jnp.float32)
    logit = sum_score(jnp.sum(crossed * wide_out[None, :], axis=1))
    dlogit = jax.nn.sigmoid(logit) - target
    dcrossed = dlogit[:, None] * wide_out[None, :]
    dgate_f = dcrossed * comp_f
    vectors = jnp.stack([jnp.sum(dgate_f, axis=0), jnp.sum(dlogit[:, None] * crossed, axis=0)])
    dgate = dgate_f.astype(jnp.bfloat16)
    grad_up = contract_rows(dgate, lowrank)
    dlowrank = sum_back(jnp.dot(dgate, upper, preferred_element_type=jnp.float32)).astype(
        jnp.bfloat16
    )
    grad_down = contract_rows(compressed, dlowrank)
    dcomp = dcrossed * (gate + 1.0) + lax.dot_general(
        dlowrank, down, (((1,), (1,)), ((), ())), preferred_element_type=jnp.float32
    )
    return (dcomp.astype(jnp.bfloat16), grad_down, grad_up, vectors)


def shards_spread(features, compress, top_down, top_up, top_bias, out_weight, labels):
    local_towers, feat_rows, batch = features.shape
    comp_width = compress.shape[2]
    group_width = local_towers * comp_width
    mine = batch // lax.axis_size("member")
    member_idx = lax.axis_index("member")
    tower_idx = lax.axis_index("tower")
    block = features
    term = jnp.einsum("kfn,kfc->nkc", block, compress, preferred_element_type=jnp.float32)
    local = lax.psum_scatter(
        term.reshape(mine * lax.axis_size("member"), group_width),
        "member",
        scatter_dimension=0,
        tiled=True,
    ).astype(jnp.bfloat16)
    offset = tower_idx * group_width
    down_t = lax.dynamic_slice_in_dim(top_down, offset, group_width, 0)
    upper_t = lax.dynamic_slice_in_dim(top_up, offset, group_width, 0)
    bias_t = lax.dynamic_slice_in_dim(top_bias, offset, group_width, 0)
    wout_t = lax.dynamic_slice_in_dim(out_weight, offset, group_width, 0)
    target = lax.dynamic_slice_in_dim(labels, member_idx * mine, mine, 0).astype(jnp.float32)
    dcomp, grad_down, grad_up, vectors = cross_top(
        local,
        down_t,
        upper_t,
        bias_t,
        wout_t,
        target,
        lambda value: lax.psum(value, "tower"),
        lambda value: lax.psum(value, "tower"),
        lambda value: lax.psum(value, "tower"),
    )
    grad_down, grad_up, vectors = (
        lax.psum_scatter(grad_down, "member", scatter_dimension=0, tiled=True),
        lax.psum_scatter(grad_up, "member", scatter_dimension=0, tiled=True),
        lax.psum_scatter(vectors, "member", scatter_dimension=1, tiled=True),
    )
    piece = lax.all_gather(dcomp, "member", axis=0, tiled=True)
    count = piece.shape[0]
    block = features
    split_piece = piece.reshape(count, local_towers, comp_width)
    grad_w = jnp.einsum("kfn,nkc->kfc", block, split_piece, preferred_element_type=jnp.float32)
    column = jnp.einsum("kfc,nkc->kfn", compress, split_piece, preferred_element_type=jnp.float32)
    grad_x = column
    grad_w, grad_x = (grad_w, grad_x)
    return (grad_w, grad_x.astype(jnp.bfloat16), grad_down, grad_up, vectors)


F32, BF16 = jnp.float32, jnp.bfloat16
VMEM = pl.BlockSpec(memory_space=pltpu.VMEM)
ANY = pl.BlockSpec(memory_space=pl.ANY)
CHUNKS = 4


def nt(left, right):
    return lax.dot_general(left, right, (((1,), (1,)), ((), ())), preferred_element_type=F32)


def exchange(value, tower_bit, member_bit):
    towers, members = lax.axis_size("tower"), lax.axis_size("member")
    pairs = [
        (t * members + m, (t ^ tower_bit) * members + (m ^ member_bit))
        for t in range(towers)
        for m in range(members)
    ]
    return lax.ppermute(value, ("tower", "member"), pairs)


def term_kernel(flip, feat_hbm, comp_hbm, out, feat, comp, sems):
    which = lax.rem(lax.axis_index("member") + flip, 2)
    rows = comp.shape[1]
    load_feat = pltpu.make_async_copy(feat_hbm.at[which], feat, sems.at[2])
    loads = [
        pltpu.make_async_copy(
            comp_hbm.at[which, pl.ds(i * rows, rows)], comp.at[i], sems.at[i]
        )
        for i in range(2)
    ]
    load_feat.start()
    for load in loads:
        load.start()
    load_feat.wait()
    total = None
    for i in range(2):
        loads[i].wait()
        part = jnp.dot(feat[:, i * rows : (i + 1) * rows], comp[i], preferred_element_type=F32)
        total = part if total is None else total + part
    out[...] = total


def term(flip, feat_t, compress):
    _, batch, rows = feat_t.shape
    width = compress.shape[2]
    return pl.pallas_call(
        lambda *refs: term_kernel(flip, *refs),
        out_shape=jax.ShapeDtypeStruct((batch, width), F32),
        in_specs=[ANY, ANY],
        out_specs=VMEM,
        scratch_shapes=[
            pltpu.VMEM((batch, rows), BF16),
            pltpu.VMEM((2, rows // 2, width), BF16),
            pltpu.SemaphoreType.DMA((3,)),
        ],
        compiler_params=pltpu.CompilerParams(vmem_limit_bytes=2 << 20),
        cost_estimate=pl.CostEstimate(
            flops=2 * batch * rows * width, bytes_accessed=2 * rows * (width + batch), transcendentals=0
        ),
    )(
        pltpu.with_memory_space_constraint(feat_t, pltpu.HBM),
        pltpu.with_memory_space_constraint(compress, pltpu.HBM),
    )


def top_kernel(
    mine, side_piece, tower_piece, both_piece, down, upper, bias, wout, labels_hbm, feat, comp,
    grad_w_hbm, grad_x_hbm, grad_down_hbm, grad_up_hbm, vectors_hbm,
    compressed, gates, wide, labels, grad_w, grad_x, up_square, down_square, vectors, sems,
):
    tower, member = lax.axis_index("tower"), lax.axis_index("member")
    side = lax.rem(member, 2)
    batch, width = mine.shape
    pieces = compressed.shape[0]
    load_labels = pltpu.make_async_copy(labels_hbm, labels, sems.at[CHUNKS + 5])
    load_labels.start()
    compressed[2 * tower + side] = mine[...]
    compressed[2 * tower + 1 - side] = side_piece[...]
    compressed[2 * (1 - tower) + side] = tower_piece[...]
    compressed[2 * (1 - tower) + 1 - side] = both_piece[...]
    block = lambda j: slice(j * width, (j + 1) * width)
    summed = lambda parts: functools.reduce(jnp.add, parts)

    low = summed(
        jnp.dot(compressed[j], down[block(j), :], preferred_element_type=F32)
        for j in range(pieces)
    ).astype(BF16)
    weighted, scores = [], []
    for j in range(pieces):
        gate = nt(low, upper[block(j), :]) + bias[:, block(j)]
        gates[j] = gate
        out_row = wout[:, block(j)].astype(F32)
        wide[j] = out_row
        comp_f = compressed[j].astype(F32)
        weighted.append((comp_f * out_row).astype(BF16))
        scores.append((comp_f * gate + comp_f) * out_row)
    logit = jnp.sum(summed(scores), axis=1, keepdims=True)
    back = summed(
        jnp.dot(weighted[j], upper[block(j), :], preferred_element_type=F32)
        for j in range(pieces)
    )
    back_low = back.astype(BF16)
    slopes = []
    for k in range(2):
        j = 2 * tower + k
        rows = pl.ds(pl.multiple_of(j * width, width), width)
        slopes.append(wide[j] * (gates[j] + 1.0) + nt(back_low, down[rows, :]))
    row = lax.broadcasted_iota(jnp.int32, (batch, batch), 0)
    col = lax.broadcasted_iota(jnp.int32, (batch, batch), 1)
    load_labels.wait()
    target = jnp.sum(jnp.where(row == col, labels[...].astype(F32), 0.0), axis=1, keepdims=True)
    dlogit = 1.0 / (1.0 + jnp.exp(-logit)) - target

    stores = []

    def send(source, target):
        stores.append(pltpu.make_async_copy(source, target, sems.at[len(stores)]))
        stores[-1].start()

    size = grad_w.shape[1]
    per_tower = CHUNKS // 2
    dcomps = [(dlogit * slope).astype(BF16) for slope in slopes]
    for i in range(CHUNKS):
        k, part = i // per_tower, i % per_tower
        grad_w[i] = contract_rows(feat[k, :, part * size : (part + 1) * size], dcomps[k])
        send(grad_w.at[i], grad_w_hbm.at[k, pl.ds(part * size, size)])
    for k in range(2):
        grad_x[k] = nt(dcomps[k], comp[k]).astype(BF16)
        send(grad_x.at[k], grad_x_hbm.at[k])

    count = grad_down_hbm.shape[0]
    first = (tower * lax.axis_size("member") + member) * count
    own = lax.div(first, width)
    offset = pl.multiple_of(lax.rem(first, width), count)
    comp_f = compressed[own].astype(F32)
    dgate_f = dlogit * wide[own] * comp_f
    crossed = comp_f * gates[own] + comp_f
    up_square[...] = contract_rows(dgate_f.astype(BF16), low)
    send(up_square.at[pl.ds(offset, count)], grad_up_hbm)
    down_square[...] = contract_rows(compressed[own], (dlogit * back).astype(BF16))
    send(down_square.at[pl.ds(offset, count)], grad_down_hbm)
    sums = jnp.concatenate(
        [
            jnp.sum(dgate_f, axis=0, keepdims=True),
            jnp.sum(dlogit * crossed, axis=0, keepdims=True),
            jnp.zeros((6, width), F32),
        ],
        axis=0,
    )
    vectors[...] = pltpu.roll(sums, width - offset, 1)[0:2, 0:count]
    send(vectors, vectors_hbm)
    for store in stores:
        store.wait()


def shards_doubling(features, compress, top_down, top_up, top_bias, out_weight, labels):
    local_towers, feat_rows, batch = features.shape
    width = compress.shape[2]
    rank = top_down.shape[1]
    members = lax.axis_size("member")
    top = top_down.shape[0]
    count = top // (2 * members)
    pieces = top // width
    feat_t = jnp.swapaxes(features, 1, 2)
    total = term(0, feat_t, compress) + exchange(term(1, feat_t, compress), 0, 1)
    strides = [1 << bit for bit in range(1, members.bit_length() - 1)]
    if len(strides) > 1:
        one, two = strides.pop(0), strides.pop(0)
        total = total + sum(exchange(total, 0, bits) for bits in (one, two, one | two))
    for stride in strides:
        total = total + exchange(total, 0, stride)
    mine = total.astype(BF16)
    near = lambda value: pltpu.with_memory_space_constraint(value, pltpu.VMEM)
    grad_w, grad_x, grad_down, grad_up, vectors = pl.pallas_call(
        top_kernel,
        out_shape=(
            jax.ShapeDtypeStruct((local_towers, feat_rows, width), F32),
            jax.ShapeDtypeStruct((local_towers, batch, feat_rows), BF16),
            jax.ShapeDtypeStruct((count, rank), F32),
            jax.ShapeDtypeStruct((count, rank), F32),
            jax.ShapeDtypeStruct((2, count), F32),
        ),
        in_specs=[VMEM] * 8 + [ANY, VMEM, VMEM],
        out_specs=(ANY,) * 5,
        scratch_shapes=[
            pltpu.VMEM((pieces, batch, width), BF16),
            pltpu.VMEM((pieces, batch, width), F32),
            pltpu.VMEM((pieces, 1, width), F32),
            pltpu.VMEM((1, batch), labels.dtype),
            pltpu.VMEM((CHUNKS, local_towers * feat_rows // CHUNKS, width), F32),
            pltpu.VMEM((local_towers, batch, feat_rows), BF16),
            pltpu.VMEM((width, rank), F32),
            pltpu.VMEM((width, rank), F32),
            pltpu.VMEM((2, count), F32),
            pltpu.SemaphoreType.DMA((CHUNKS + 6,)),
        ],
        compiler_params=pltpu.CompilerParams(vmem_limit_bytes=8 << 20),
        cost_estimate=pl.CostEstimate(
            flops=10 * batch * top * rank, bytes_accessed=4 << 20, transcendentals=batch
        ),
    )(
        near(mine),
        near(exchange(mine, 0, 1)),
        near(exchange(mine, 1, 0)),
        near(exchange(mine, 1, 1)),
        near(top_down),
        near(top_up),
        near(top_bias.reshape(1, top)),
        near(out_weight.reshape(1, top)),
        pltpu.with_memory_space_constraint(labels.reshape(1, batch), pltpu.HBM),
        near(feat_t),
        near(compress),
    )
    return grad_w, jnp.swapaxes(grad_x, 1, 2), grad_down, grad_up, vectors


def shards(features, compress, top_down, *rest):
    towers, members = lax.axis_size("tower"), lax.axis_size("member")
    small = towers == 2 and features.shape[0] == 2 and features.shape[2] <= 128
    power = members > 1 and members & (members - 1) == 0
    body = shards_doubling if small and power else shards_spread
    return body(features, compress, top_down, *rest)


def solution(mesh):
    placed = (P("tower", "member", None), P("tower", "member", None), P(), P(), P(), P(), P())
    return jax.shard_map(
        shards,
        mesh=mesh,
        in_specs=placed,
        out_specs=(
            P("tower", "member", None),
            P("tower", "member", None),
            P(("tower", "member"), None),
            P(("tower", "member"), None),
            P(None, ("tower", "member")),
        ),
        check_vma=False,
    )
```

```python
import functools

import jax
import jax.numpy as jnp
from jax import lax
from jax.experimental import pallas as pl
from jax.experimental.pallas import tpu as pltpu
from jax.sharding import PartitionSpec as P


def contract_rows(left, right):
    return lax.dot_general(
        left, right, (((0,), (0,)), ((), ())), preferred_element_type=jnp.float32
    )


def cross_top(compressed, down, upper, bias, wout, target, sum_low, sum_score, sum_back):
    lowrank = sum_low(jnp.dot(compressed, down, preferred_element_type=jnp.float32)).astype(
        jnp.bfloat16
    )
    gate = (
        lax.dot_general(
            lowrank, upper, (((1,), (1,)), ((), ())), preferred_element_type=jnp.float32
        )
        + bias
    )
    comp_f = compressed.astype(jnp.float32)
    crossed = comp_f * gate + comp_f
    wide_out = wout.astype(jnp.float32)
    logit = sum_score(jnp.sum(crossed * wide_out[None, :], axis=1))
    dlogit = jax.nn.sigmoid(logit) - target
    dcrossed = dlogit[:, None] * wide_out[None, :]
    dgate_f = dcrossed * comp_f
    vectors = jnp.stack([jnp.sum(dgate_f, axis=0), jnp.sum(dlogit[:, None] * crossed, axis=0)])
    dgate = dgate_f.astype(jnp.bfloat16)
    grad_up = contract_rows(dgate, lowrank)
    dlowrank = sum_back(jnp.dot(dgate, upper, preferred_element_type=jnp.float32)).astype(
        jnp.bfloat16
    )
    grad_down = contract_rows(compressed, dlowrank)
    dcomp = dcrossed * (gate + 1.0) + lax.dot_general(
        dlowrank, down, (((1,), (1,)), ((), ())), preferred_element_type=jnp.float32
    )
    return (dcomp.astype(jnp.bfloat16), grad_down, grad_up, vectors)


def shards_spread(features, compress, top_down, top_up, top_bias, out_weight, labels):
    local_towers, feat_rows, batch = features.shape
    comp_width = compress.shape[2]
    group_width = local_towers * comp_width
    mine = batch // lax.axis_size("member")
    member_idx = lax.axis_index("member")
    tower_idx = lax.axis_index("tower")
    block = features
    term = jnp.einsum("kfn,kfc->nkc", block, compress, preferred_element_type=jnp.float32)
    local = lax.psum_scatter(
        term.reshape(mine * lax.axis_size("member"), group_width),
        "member",
        scatter_dimension=0,
        tiled=True,
    ).astype(jnp.bfloat16)
    offset = tower_idx * group_width
    down_t = lax.dynamic_slice_in_dim(top_down, offset, group_width, 0)
    upper_t = lax.dynamic_slice_in_dim(top_up, offset, group_width, 0)
    bias_t = lax.dynamic_slice_in_dim(top_bias, offset, group_width, 0)
    wout_t = lax.dynamic_slice_in_dim(out_weight, offset, group_width, 0)
    target = lax.dynamic_slice_in_dim(labels, member_idx * mine, mine, 0).astype(jnp.float32)
    dcomp, grad_down, grad_up, vectors = cross_top(
        local,
        down_t,
        upper_t,
        bias_t,
        wout_t,
        target,
        lambda value: lax.psum(value, "tower"),
        lambda value: lax.psum(value, "tower"),
        lambda value: lax.psum(value, "tower"),
    )
    grad_down, grad_up, vectors = (
        lax.psum_scatter(grad_down, "member", scatter_dimension=0, tiled=True),
        lax.psum_scatter(grad_up, "member", scatter_dimension=0, tiled=True),
        lax.psum_scatter(vectors, "member", scatter_dimension=1, tiled=True),
    )
    piece = lax.all_gather(dcomp, "member", axis=0, tiled=True)
    count = piece.shape[0]
    block = features
    split_piece = piece.reshape(count, local_towers, comp_width)
    grad_w = jnp.einsum("kfn,nkc->kfc", block, split_piece, preferred_element_type=jnp.float32)
    column = jnp.einsum("kfc,nkc->kfn", compress, split_piece, preferred_element_type=jnp.float32)
    grad_x = column
    grad_w, grad_x = (grad_w, grad_x)
    return (grad_w, grad_x.astype(jnp.bfloat16), grad_down, grad_up, vectors)


F32, BF16 = jnp.float32, jnp.bfloat16
VMEM = pl.BlockSpec(memory_space=pltpu.VMEM)
ANY = pl.BlockSpec(memory_space=pl.ANY)
CHUNKS = 4


def nt(left, right):
    return lax.dot_general(left, right, (((1,), (1,)), ((), ())), preferred_element_type=F32)


def side_of(member):
    return lax.rem(member, 2)


def exchange(value, tower_bit, member_bit):
    towers, members = lax.axis_size("tower"), lax.axis_size("member")
    pairs = [
        (t * members + m, (t ^ tower_bit) * members + (m ^ member_bit))
        for t in range(towers)
        for m in range(members)
    ]
    return lax.ppermute(value, ("tower", "member"), pairs)


def sent_kernel(feat_hbm, comp_hbm, out, feat, comp, sems):
    which = 1 - side_of(lax.axis_index("member"))
    parts, rows, _ = comp.shape
    load_feat = pltpu.make_async_copy(feat_hbm.at[which], feat, sems.at[parts])
    loads = [
        pltpu.make_async_copy(
            comp_hbm.at[which, pl.ds(i * rows, rows)], comp.at[i], sems.at[i]
        )
        for i in range(parts)
    ]
    load_feat.start()
    for load in loads:
        load.start()
    load_feat.wait()
    total = None
    for i in range(parts):
        loads[i].wait()
        part = jnp.dot(feat[:, i * rows : (i + 1) * rows], comp[i], preferred_element_type=F32)
        total = part if total is None else total + part
    out[...] = total


def kept_kernel(feat, comp, labels_hbm, out, target, labels, sem):
    which = side_of(lax.axis_index("member"))
    batch = feat.shape[1]
    load_labels = pltpu.make_async_copy(labels_hbm, labels, sem)
    load_labels.start()
    out[...] = jnp.dot(feat[which], comp[which], preferred_element_type=F32)
    load_labels.wait()
    row = lax.broadcasted_iota(jnp.int32, (batch, batch), 0)
    col = lax.broadcasted_iota(jnp.int32, (batch, batch), 1)
    target[...] = jnp.sum(
        jnp.where(row == col, labels[...].astype(F32), 0.0), axis=1, keepdims=True
    )


def near(value):
    return pltpu.with_memory_space_constraint(value, pltpu.VMEM)


def far(value):
    return pltpu.with_memory_space_constraint(value, pltpu.HBM)


def terms(feat_t, compress, labels):
    _, batch, rows = feat_t.shape
    width = compress.shape[2]
    parts = 2
    cost = pl.CostEstimate(
        flops=2 * batch * rows * width, bytes_accessed=2 * rows * (width + batch), transcendentals=0
    )
    limit = pltpu.CompilerParams(vmem_limit_bytes=2 << 20)
    sent = pl.pallas_call(
        sent_kernel,
        out_shape=jax.ShapeDtypeStruct((batch, width), F32),
        in_specs=[ANY, ANY],
        out_specs=VMEM,
        scratch_shapes=[
            pltpu.VMEM((batch, rows), BF16),
            pltpu.VMEM((parts, rows // parts, width), BF16),
            pltpu.SemaphoreType.DMA((parts + 1,)),
        ],
        compiler_params=limit,
        cost_estimate=cost,
    )(far(feat_t), far(compress))
    kept, target = pl.pallas_call(
        kept_kernel,
        out_shape=(
            jax.ShapeDtypeStruct((batch, width), F32),
            jax.ShapeDtypeStruct((batch, 1), F32),
        ),
        in_specs=[VMEM, VMEM, ANY],
        out_specs=(VMEM, VMEM),
        scratch_shapes=[pltpu.VMEM((1, batch), labels.dtype), pltpu.SemaphoreType.DMA],
        compiler_params=limit,
        cost_estimate=cost,
    )(near(feat_t), near(compress), far(labels.reshape(1, batch)))
    return sent, kept, target


def top_kernel(
    mine, side_piece, tower_piece, both_piece, down, upper, bias, wout, target, feat, comp,
    grad_w_hbm, grad_x_hbm, grad_down_hbm, grad_up_hbm, vectors_hbm,
    compressed, gates, wide, grad_w, grad_x, up_square, down_square, vectors, sems,
):
    tower, member = lax.axis_index("tower"), lax.axis_index("member")
    side = side_of(member)
    batch, width = mine.shape
    pieces = compressed.shape[0]
    compressed[2 * tower + side] = mine[...]
    compressed[2 * tower + 1 - side] = side_piece[...]
    compressed[2 * (1 - tower) + side] = tower_piece[...]
    compressed[2 * (1 - tower) + 1 - side] = both_piece[...]
    block = lambda j: slice(j * width, (j + 1) * width)
    summed = lambda parts: functools.reduce(jnp.add, parts)

    low = summed(
        jnp.dot(compressed[j], down[block(j), :], preferred_element_type=F32)
        for j in range(pieces)
    ).astype(BF16)
    weighted = [
        (compressed[j].astype(F32) * wout[:, block(j)].astype(F32)).astype(BF16)
        for j in range(pieces)
    ]
    back = summed(
        jnp.dot(weighted[j], upper[block(j), :], preferred_element_type=F32)
        for j in range(pieces)
    )
    back_low = back.astype(BF16)
    scores = []
    for j in range(pieces):
        gate = nt(low, upper[block(j), :]) + bias[:, block(j)]
        gates[j] = gate
        out_row = wout[:, block(j)].astype(F32)
        wide[j] = out_row
        comp_f = compressed[j].astype(F32)
        scores.append((comp_f * gate + comp_f) * out_row)
    logit = jnp.sum(summed(scores), axis=1, keepdims=True)
    slopes = []
    for k in range(2):
        j = 2 * tower + k
        rows = pl.ds(pl.multiple_of(j * width, width), width)
        slopes.append(wide[j] * (gates[j] + 1.0) + nt(back_low, down[rows, :]))
    dlogit = 1.0 / (1.0 + jnp.exp(-logit)) - target[...]

    stores = []

    def send(source, target):
        stores.append(pltpu.make_async_copy(source, target, sems.at[len(stores)]))
        stores[-1].start()

    size = grad_w.shape[1]
    per_tower = CHUNKS // 2
    dcomps = [(dlogit * slope).astype(BF16) for slope in slopes]
    for i in range(CHUNKS):
        k, part = i // per_tower, i % per_tower
        grad_w[i] = contract_rows(feat[k, :, part * size : (part + 1) * size], dcomps[k])
        send(grad_w.at[i], grad_w_hbm.at[k, pl.ds(part * size, size)])
    for k in range(2):
        grad_x[k] = nt(dcomps[k], comp[k]).astype(BF16)
        send(grad_x.at[k], grad_x_hbm.at[k])

    count = grad_down_hbm.shape[0]
    first = (tower * lax.axis_size("member") + member) * count
    own = lax.div(first, width)
    offset = pl.multiple_of(lax.rem(first, width), count)
    comp_f = compressed[own].astype(F32)
    dgate_f = dlogit * wide[own] * comp_f
    crossed = comp_f * gates[own] + comp_f
    up_square[...] = contract_rows(dgate_f.astype(BF16), low)
    send(up_square.at[pl.ds(offset, count)], grad_up_hbm)
    down_square[...] = contract_rows(compressed[own], (dlogit * back).astype(BF16))
    send(down_square.at[pl.ds(offset, count)], grad_down_hbm)
    sums = jnp.concatenate(
        [
            jnp.sum(dgate_f, axis=0, keepdims=True),
            jnp.sum(dlogit * crossed, axis=0, keepdims=True),
            jnp.zeros((6, width), F32),
        ],
        axis=0,
    )
    vectors[...] = pltpu.roll(sums, width - offset, 1)[0:2, 0:count]
    send(vectors, vectors_hbm)
    for store in stores:
        store.wait()


def shards_doubling(features, compress, top_down, top_up, top_bias, out_weight, labels):
    local_towers, feat_rows, batch = features.shape
    width = compress.shape[2]
    rank = top_down.shape[1]
    members = lax.axis_size("member")
    top = top_down.shape[0]
    count = top // (2 * members)
    pieces = top // width
    feat_t = jnp.swapaxes(features, 1, 2)
    sent, kept, target = terms(feat_t, compress, labels)
    total = kept + exchange(sent, 0, 1)
    strides = [1 << bit for bit in range(1, members.bit_length() - 1)]
    if len(strides) > 1:
        one, two = strides.pop(0), strides.pop(0)
        total = total + sum(exchange(total, 0, bits) for bits in (one, two, one | two))
    for stride in strides:
        total = total + exchange(total, 0, stride)
    mine = total.astype(BF16)
    grad_w, grad_x, grad_down, grad_up, vectors = pl.pallas_call(
        top_kernel,
        out_shape=(
            jax.ShapeDtypeStruct((local_towers, feat_rows, width), F32),
            jax.ShapeDtypeStruct((local_towers, batch, feat_rows), BF16),
            jax.ShapeDtypeStruct((count, rank), F32),
            jax.ShapeDtypeStruct((count, rank), F32),
            jax.ShapeDtypeStruct((2, count), F32),
        ),
        in_specs=[VMEM] * 11,
        out_specs=(ANY,) * 5,
        scratch_shapes=[
            pltpu.VMEM((pieces, batch, width), BF16),
            pltpu.VMEM((pieces, batch, width), F32),
            pltpu.VMEM((pieces, 1, width), F32),
            pltpu.VMEM((CHUNKS, local_towers * feat_rows // CHUNKS, width), F32),
            pltpu.VMEM((local_towers, batch, feat_rows), BF16),
            pltpu.VMEM((width, rank), F32),
            pltpu.VMEM((width, rank), F32),
            pltpu.VMEM((2, count), F32),
            pltpu.SemaphoreType.DMA((CHUNKS + 5,)),
        ],
        compiler_params=pltpu.CompilerParams(vmem_limit_bytes=8 << 20),
        cost_estimate=pl.CostEstimate(
            flops=10 * batch * top * rank, bytes_accessed=4 << 20, transcendentals=batch
        ),
    )(
        near(mine),
        near(exchange(mine, 0, 1)),
        near(exchange(mine, 1, 0)),
        near(exchange(mine, 1, 1)),
        near(top_down),
        near(top_up),
        near(top_bias.reshape(1, top)),
        near(out_weight.reshape(1, top)),
        near(target),
        near(feat_t),
        near(compress),
    )
    return grad_w, jnp.swapaxes(grad_x, 1, 2), grad_down, grad_up, vectors


def shards(features, compress, top_down, *rest):
    towers, members = lax.axis_size("tower"), lax.axis_size("member")
    small = towers == 2 and features.shape[0] == 2 and features.shape[2] <= 128
    power = members > 1 and members & (members - 1) == 0
    body = shards_doubling if small and power else shards_spread
    return body(features, compress, top_down, *rest)


def solution(mesh):
    placed = (P("tower", "member", None), P("tower", "member", None), P(), P(), P(), P(), P())
    return jax.shard_map(
        shards,
        mesh=mesh,
        in_specs=placed,
        out_specs=(
            P("tower", "member", None),
            P("tower", "member", None),
            P(("tower", "member"), None),
            P(("tower", "member"), None),
            P(None, ("tower", "member")),
        ),
        check_vma=False,
    )
```

```python
import functools

import jax
import jax.numpy as jnp
from jax import lax
from jax.experimental import pallas as pl
from jax.experimental.pallas import tpu as pltpu
from jax.sharding import PartitionSpec as P


def contract_rows(left, right):
    return lax.dot_general(
        left, right, (((0,), (0,)), ((), ())), preferred_element_type=jnp.float32
    )


def cross_top(compressed, down, upper, bias, wout, target, sum_low, sum_score, sum_back):
    lowrank = sum_low(jnp.dot(compressed, down, preferred_element_type=jnp.float32)).astype(
        jnp.bfloat16
    )
    gate = (
        lax.dot_general(
            lowrank, upper, (((1,), (1,)), ((), ())), preferred_element_type=jnp.float32
        )
        + bias
    )
    comp_f = compressed.astype(jnp.float32)
    crossed = comp_f * gate + comp_f
    wide_out = wout.astype(jnp.float32)
    logit = sum_score(jnp.sum(crossed * wide_out[None, :], axis=1))
    dlogit = jax.nn.sigmoid(logit) - target
    dcrossed = dlogit[:, None] * wide_out[None, :]
    dgate_f = dcrossed * comp_f
    vectors = jnp.stack([jnp.sum(dgate_f, axis=0), jnp.sum(dlogit[:, None] * crossed, axis=0)])
    dgate = dgate_f.astype(jnp.bfloat16)
    grad_up = contract_rows(dgate, lowrank)
    dlowrank = sum_back(jnp.dot(dgate, upper, preferred_element_type=jnp.float32)).astype(
        jnp.bfloat16
    )
    grad_down = contract_rows(compressed, dlowrank)
    dcomp = dcrossed * (gate + 1.0) + lax.dot_general(
        dlowrank, down, (((1,), (1,)), ((), ())), preferred_element_type=jnp.float32
    )
    return (dcomp.astype(jnp.bfloat16), grad_down, grad_up, vectors)


def shards_spread(features, compress, top_down, top_up, top_bias, out_weight, labels):
    local_towers, feat_rows, batch = features.shape
    comp_width = compress.shape[2]
    group_width = local_towers * comp_width
    mine = batch // lax.axis_size("member")
    member_idx = lax.axis_index("member")
    tower_idx = lax.axis_index("tower")
    block = features
    term = jnp.einsum("kfn,kfc->nkc", block, compress, preferred_element_type=jnp.float32)
    local = lax.psum_scatter(
        term.reshape(mine * lax.axis_size("member"), group_width),
        "member",
        scatter_dimension=0,
        tiled=True,
    ).astype(jnp.bfloat16)
    offset = tower_idx * group_width
    down_t = lax.dynamic_slice_in_dim(top_down, offset, group_width, 0)
    upper_t = lax.dynamic_slice_in_dim(top_up, offset, group_width, 0)
    bias_t = lax.dynamic_slice_in_dim(top_bias, offset, group_width, 0)
    wout_t = lax.dynamic_slice_in_dim(out_weight, offset, group_width, 0)
    target = lax.dynamic_slice_in_dim(labels, member_idx * mine, mine, 0).astype(jnp.float32)
    dcomp, grad_down, grad_up, vectors = cross_top(
        local,
        down_t,
        upper_t,
        bias_t,
        wout_t,
        target,
        lambda value: lax.psum(value, "tower"),
        lambda value: lax.psum(value, "tower"),
        lambda value: lax.psum(value, "tower"),
    )
    grad_down, grad_up, vectors = (
        lax.psum_scatter(grad_down, "member", scatter_dimension=0, tiled=True),
        lax.psum_scatter(grad_up, "member", scatter_dimension=0, tiled=True),
        lax.psum_scatter(vectors, "member", scatter_dimension=1, tiled=True),
    )
    piece = lax.all_gather(dcomp, "member", axis=0, tiled=True)
    count = piece.shape[0]
    block = features
    split_piece = piece.reshape(count, local_towers, comp_width)
    grad_w = jnp.einsum("kfn,nkc->kfc", block, split_piece, preferred_element_type=jnp.float32)
    column = jnp.einsum("kfc,nkc->kfn", compress, split_piece, preferred_element_type=jnp.float32)
    grad_x = column
    grad_w, grad_x = (grad_w, grad_x)
    return (grad_w, grad_x.astype(jnp.bfloat16), grad_down, grad_up, vectors)


F32, BF16 = jnp.float32, jnp.bfloat16
VMEM = pl.BlockSpec(memory_space=pltpu.VMEM)
ANY = pl.BlockSpec(memory_space=pl.ANY)
CHUNKS = 4


def nt(left, right):
    return lax.dot_general(left, right, (((1,), (1,)), ((), ())), preferred_element_type=F32)


def side_of(member):
    return lax.rem(member, 2)


def exchange(value, tower_bit, member_bit):
    towers, members = lax.axis_size("tower"), lax.axis_size("member")
    pairs = [
        (t * members + m, (t ^ tower_bit) * members + (m ^ member_bit))
        for t in range(towers)
        for m in range(members)
    ]
    return lax.ppermute(value, ("tower", "member"), pairs)


def sent_kernel(feat_hbm, comp_hbm, out, feat, comp, sems):
    which = 1 - side_of(lax.axis_index("member"))
    parts, rows, _ = comp.shape
    load_feat = pltpu.make_async_copy(feat_hbm.at[which], feat, sems.at[parts])
    loads = [
        pltpu.make_async_copy(
            comp_hbm.at[which, pl.ds(i * rows, rows)], comp.at[i], sems.at[i]
        )
        for i in range(parts)
    ]
    load_feat.start()
    for load in loads:
        load.start()
    load_feat.wait()
    total = None
    for i in range(parts):
        loads[i].wait()
        part = jnp.dot(feat[:, i * rows : (i + 1) * rows], comp[i], preferred_element_type=F32)
        total = part if total is None else total + part
    out[...] = total


def kept_kernel(feat, comp, labels_hbm, out, target, labels, sem):
    which = side_of(lax.axis_index("member"))
    batch = feat.shape[1]
    load_labels = pltpu.make_async_copy(labels_hbm, labels, sem)
    load_labels.start()
    out[...] = jnp.dot(feat[which], comp[which], preferred_element_type=F32)
    load_labels.wait()
    row = lax.broadcasted_iota(jnp.int32, (batch, batch), 0)
    col = lax.broadcasted_iota(jnp.int32, (batch, batch), 1)
    target[...] = jnp.sum(
        jnp.where(row == col, labels[...].astype(F32), 0.0), axis=1, keepdims=True
    )


def near(value):
    return pltpu.with_memory_space_constraint(value, pltpu.VMEM)


def far(value):
    return pltpu.with_memory_space_constraint(value, pltpu.HBM)


def terms(feat_t, compress, labels):
    _, batch, rows = feat_t.shape
    width = compress.shape[2]
    parts = 2
    cost = pl.CostEstimate(
        flops=2 * batch * rows * width, bytes_accessed=2 * rows * (width + batch), transcendentals=0
    )
    limit = pltpu.CompilerParams(vmem_limit_bytes=2 << 20)
    sent = pl.pallas_call(
        sent_kernel,
        out_shape=jax.ShapeDtypeStruct((batch, width), F32),
        in_specs=[ANY, ANY],
        out_specs=VMEM,
        scratch_shapes=[
            pltpu.VMEM((batch, rows), BF16),
            pltpu.VMEM((parts, rows // parts, width), BF16),
            pltpu.SemaphoreType.DMA((parts + 1,)),
        ],
        compiler_params=limit,
        cost_estimate=cost,
    )(far(feat_t), far(compress))
    kept, target = pl.pallas_call(
        kept_kernel,
        out_shape=(
            jax.ShapeDtypeStruct((batch, width), F32),
            jax.ShapeDtypeStruct((batch, 1), F32),
        ),
        in_specs=[VMEM, VMEM, ANY],
        out_specs=(VMEM, VMEM),
        scratch_shapes=[pltpu.VMEM((1, batch), labels.dtype), pltpu.SemaphoreType.DMA],
        compiler_params=limit,
        cost_estimate=cost,
    )(near(feat_t), near(compress), far(labels.reshape(1, batch)))
    return sent, kept, target


def top_kernel(
    mine, side_piece, tower_piece, both_piece, down, upper, bias, wout, target, feat, comp,
    grad_w_hbm, grad_x_hbm, grad_down_hbm, grad_up_hbm, vectors_hbm,
    compressed, gates, wide, grad_w, grad_x, up_square, down_square, vectors, sems,
):
    tower, member = lax.axis_index("tower"), lax.axis_index("member")
    side = side_of(member)
    batch, width = mine.shape
    pieces = compressed.shape[0]
    compressed[2 * tower + side] = mine[...]
    compressed[2 * tower + 1 - side] = side_piece[...]
    compressed[2 * (1 - tower) + side] = tower_piece[...]
    compressed[2 * (1 - tower) + 1 - side] = both_piece[...]
    block = lambda j: slice(j * width, (j + 1) * width)
    summed = lambda parts: functools.reduce(jnp.add, parts)

    low = summed(
        jnp.dot(compressed[j], down[block(j), :], preferred_element_type=F32)
        for j in range(pieces)
    ).astype(BF16)
    weighted = [
        (compressed[j].astype(F32) * wout[:, block(j)].astype(F32)).astype(BF16)
        for j in range(pieces)
    ]
    back = summed(
        jnp.dot(weighted[j], upper[block(j), :], preferred_element_type=F32)
        for j in range(pieces)
    )
    back_low = back.astype(BF16)
    scores = []
    for j in range(pieces):
        gate = nt(low, upper[block(j), :]) + bias[:, block(j)]
        gates[j] = gate
        out_row = wout[:, block(j)].astype(F32)
        wide[j] = out_row
        comp_f = compressed[j].astype(F32)
        scores.append((comp_f * gate + comp_f) * out_row)
    logit = jnp.sum(summed(scores), axis=1, keepdims=True)
    slopes = []
    for k in range(2):
        j = 2 * tower + k
        rows = pl.ds(pl.multiple_of(j * width, width), width)
        slopes.append(wide[j] * (gates[j] + 1.0) + nt(back_low, down[rows, :]))
    dlogit = 1.0 / (1.0 + jnp.exp(-logit)) - target[...]

    stores = []

    def send(source, target):
        stores.append(pltpu.make_async_copy(source, target, sems.at[len(stores)]))
        stores[-1].start()

    size = grad_w.shape[1]
    per_tower = CHUNKS // 2
    dcomps = [(dlogit * slope).astype(BF16) for slope in slopes]
    for i in range(CHUNKS):
        k, part = i // per_tower, i % per_tower
        grad_w[i] = contract_rows(feat[k, :, part * size : (part + 1) * size], dcomps[k])
        send(grad_w.at[i], grad_w_hbm.at[k, pl.ds(part * size, size)])
    for k in range(2):
        grad_x[k] = nt(dcomps[k], comp[k]).astype(BF16)
        send(grad_x.at[k], grad_x_hbm.at[k])

    count = grad_down_hbm.shape[0]
    first = (tower * lax.axis_size("member") + member) * count
    own = lax.div(first, width)
    offset = pl.multiple_of(lax.rem(first, width), count)
    comp_f = compressed[own].astype(F32)
    dgate_f = dlogit * wide[own] * comp_f
    crossed = comp_f * gates[own] + comp_f
    up_square[...] = contract_rows(dgate_f.astype(BF16), low)
    send(up_square.at[pl.ds(offset, count)], grad_up_hbm)
    down_square[...] = contract_rows(compressed[own], (dlogit * back).astype(BF16))
    send(down_square.at[pl.ds(offset, count)], grad_down_hbm)
    sums = jnp.concatenate(
        [
            jnp.sum(dgate_f, axis=0, keepdims=True),
            jnp.sum(dlogit * crossed, axis=0, keepdims=True),
            jnp.zeros((6, width), F32),
        ],
        axis=0,
    )
    vectors[...] = pltpu.roll(sums, width - offset, 1)[0:2, 0:count]
    send(vectors, vectors_hbm)
    for store in stores:
        store.wait()


def shards_doubling(features, compress, top_down, top_up, top_bias, out_weight, labels):
    local_towers, feat_rows, batch = features.shape
    width = compress.shape[2]
    rank = top_down.shape[1]
    members = lax.axis_size("member")
    top = top_down.shape[0]
    count = top // (2 * members)
    pieces = top // width
    feat_t = jnp.swapaxes(features, 1, 2)
    sent, kept, target = terms(feat_t, compress, labels)
    total = kept + exchange(sent, 0, 1)
    strides = [1 << bit for bit in range(1, members.bit_length() - 1)]
    if len(strides) > 1:
        one, two = strides.pop(0), strides.pop(0)
        total = total + sum(exchange(total, 0, bits) for bits in (one, two, one | two))
    for stride in strides:
        total = total + exchange(total.astype(BF16), 0, stride).astype(F32)
    mine = total.astype(BF16)
    grad_w, grad_x, grad_down, grad_up, vectors = pl.pallas_call(
        top_kernel,
        out_shape=(
            jax.ShapeDtypeStruct((local_towers, feat_rows, width), F32),
            jax.ShapeDtypeStruct((local_towers, batch, feat_rows), BF16),
            jax.ShapeDtypeStruct((count, rank), F32),
            jax.ShapeDtypeStruct((count, rank), F32),
            jax.ShapeDtypeStruct((2, count), F32),
        ),
        in_specs=[VMEM] * 11,
        out_specs=(ANY,) * 5,
        scratch_shapes=[
            pltpu.VMEM((pieces, batch, width), BF16),
            pltpu.VMEM((pieces, batch, width), F32),
            pltpu.VMEM((pieces, 1, width), F32),
            pltpu.VMEM((CHUNKS, local_towers * feat_rows // CHUNKS, width), F32),
            pltpu.VMEM((local_towers, batch, feat_rows), BF16),
            pltpu.VMEM((width, rank), F32),
            pltpu.VMEM((width, rank), F32),
            pltpu.VMEM((2, count), F32),
            pltpu.SemaphoreType.DMA((CHUNKS + 5,)),
        ],
        compiler_params=pltpu.CompilerParams(vmem_limit_bytes=8 << 20),
        cost_estimate=pl.CostEstimate(
            flops=10 * batch * top * rank, bytes_accessed=4 << 20, transcendentals=batch
        ),
    )(
        near(mine),
        near(exchange(mine, 0, 1)),
        near(exchange(mine, 1, 0)),
        near(exchange(mine, 1, 1)),
        near(top_down),
        near(top_up),
        near(top_bias.reshape(1, top)),
        near(out_weight.reshape(1, top)),
        near(target),
        near(feat_t),
        near(compress),
    )
    return grad_w, jnp.swapaxes(grad_x, 1, 2), grad_down, grad_up, vectors


def shards(features, compress, top_down, *rest):
    towers, members = lax.axis_size("tower"), lax.axis_size("member")
    small = towers == 2 and features.shape[0] == 2 and features.shape[2] <= 128
    power = members > 1 and members & (members - 1) == 0
    body = shards_doubling if small and power else shards_spread
    return body(features, compress, top_down, *rest)


def solution(mesh):
    placed = (P("tower", "member", None), P("tower", "member", None), P(), P(), P(), P(), P())
    return jax.shard_map(
        shards,
        mesh=mesh,
        in_specs=placed,
        out_specs=(
            P("tower", "member", None),
            P("tower", "member", None),
            P(("tower", "member"), None),
            P(("tower", "member"), None),
            P(None, ("tower", "member")),
        ),
        check_vma=False,
    )
```

```python
import functools

import jax
import jax.numpy as jnp
from jax import lax
from jax.experimental import pallas as pl
from jax.experimental.pallas import tpu as pltpu
from jax.sharding import PartitionSpec as P


def contract_rows(left, right):
    return lax.dot_general(
        left, right, (((0,), (0,)), ((), ())), preferred_element_type=jnp.float32
    )


def cross_top(compressed, down, upper, bias, wout, target, sum_low, sum_score, sum_back):
    lowrank = sum_low(jnp.dot(compressed, down, preferred_element_type=jnp.float32)).astype(
        jnp.bfloat16
    )
    gate = (
        lax.dot_general(
            lowrank, upper, (((1,), (1,)), ((), ())), preferred_element_type=jnp.float32
        )
        + bias
    )
    comp_f = compressed.astype(jnp.float32)
    crossed = comp_f * gate + comp_f
    wide_out = wout.astype(jnp.float32)
    logit = sum_score(jnp.sum(crossed * wide_out[None, :], axis=1))
    dlogit = jax.nn.sigmoid(logit) - target
    dcrossed = dlogit[:, None] * wide_out[None, :]
    dgate_f = dcrossed * comp_f
    vectors = jnp.stack([jnp.sum(dgate_f, axis=0), jnp.sum(dlogit[:, None] * crossed, axis=0)])
    dgate = dgate_f.astype(jnp.bfloat16)
    grad_up = contract_rows(dgate, lowrank)
    dlowrank = sum_back(jnp.dot(dgate, upper, preferred_element_type=jnp.float32)).astype(
        jnp.bfloat16
    )
    grad_down = contract_rows(compressed, dlowrank)
    dcomp = dcrossed * (gate + 1.0) + lax.dot_general(
        dlowrank, down, (((1,), (1,)), ((), ())), preferred_element_type=jnp.float32
    )
    return (dcomp.astype(jnp.bfloat16), grad_down, grad_up, vectors)


def shards_spread(features, compress, top_down, top_up, top_bias, out_weight, labels):
    local_towers, feat_rows, batch = features.shape
    comp_width = compress.shape[2]
    group_width = local_towers * comp_width
    mine = batch // lax.axis_size("member")
    member_idx = lax.axis_index("member")
    tower_idx = lax.axis_index("tower")
    block = features
    term = jnp.einsum("kfn,kfc->nkc", block, compress, preferred_element_type=jnp.float32)
    local = lax.psum_scatter(
        term.reshape(mine * lax.axis_size("member"), group_width),
        "member",
        scatter_dimension=0,
        tiled=True,
    ).astype(jnp.bfloat16)
    offset = tower_idx * group_width
    down_t = lax.dynamic_slice_in_dim(top_down, offset, group_width, 0)
    upper_t = lax.dynamic_slice_in_dim(top_up, offset, group_width, 0)
    bias_t = lax.dynamic_slice_in_dim(top_bias, offset, group_width, 0)
    wout_t = lax.dynamic_slice_in_dim(out_weight, offset, group_width, 0)
    target = lax.dynamic_slice_in_dim(labels, member_idx * mine, mine, 0).astype(jnp.float32)
    dcomp, grad_down, grad_up, vectors = cross_top(
        local,
        down_t,
        upper_t,
        bias_t,
        wout_t,
        target,
        lambda value: lax.psum(value, "tower"),
        lambda value: lax.psum(value, "tower"),
        lambda value: lax.psum(value, "tower"),
    )
    grad_down, grad_up, vectors = (
        lax.psum_scatter(grad_down, "member", scatter_dimension=0, tiled=True),
        lax.psum_scatter(grad_up, "member", scatter_dimension=0, tiled=True),
        lax.psum_scatter(vectors, "member", scatter_dimension=1, tiled=True),
    )
    piece = lax.all_gather(dcomp, "member", axis=0, tiled=True)
    count = piece.shape[0]
    block = features
    split_piece = piece.reshape(count, local_towers, comp_width)
    grad_w = jnp.einsum("kfn,nkc->kfc", block, split_piece, preferred_element_type=jnp.float32)
    column = jnp.einsum("kfc,nkc->kfn", compress, split_piece, preferred_element_type=jnp.float32)
    grad_x = column
    grad_w, grad_x = (grad_w, grad_x)
    return (grad_w, grad_x.astype(jnp.bfloat16), grad_down, grad_up, vectors)


F32, BF16 = jnp.float32, jnp.bfloat16
VMEM = pl.BlockSpec(memory_space=pltpu.VMEM)
ANY = pl.BlockSpec(memory_space=pl.ANY)
CHUNKS = 4


def nt(left, right):
    return lax.dot_general(left, right, (((1,), (1,)), ((), ())), preferred_element_type=F32)


def side_of(member):
    return lax.rem(member, 2)


def exchange(value, tower_bit, member_bit):
    towers, members = lax.axis_size("tower"), lax.axis_size("member")
    pairs = [
        (t * members + m, (t ^ tower_bit) * members + (m ^ member_bit))
        for t in range(towers)
        for m in range(members)
    ]
    return lax.ppermute(value, ("tower", "member"), pairs)


def sent_kernel(feat_hbm, comp_hbm, out, feat, comp, sems):
    which = 1 - side_of(lax.axis_index("member"))
    parts, rows, _ = comp.shape
    load_feat = pltpu.make_async_copy(feat_hbm.at[which], feat, sems.at[parts])
    loads = [
        pltpu.make_async_copy(
            comp_hbm.at[which, pl.ds(i * rows, rows)], comp.at[i], sems.at[i]
        )
        for i in range(parts)
    ]
    load_feat.start()
    for load in loads:
        load.start()
    load_feat.wait()
    total = None
    for i in range(parts):
        loads[i].wait()
        part = jnp.dot(feat[:, i * rows : (i + 1) * rows], comp[i], preferred_element_type=F32)
        total = part if total is None else total + part
    out[...] = total


def kept_kernel(feat, comp, labels_hbm, out, target, labels, sem):
    which = side_of(lax.axis_index("member"))
    batch = feat.shape[1]
    load_labels = pltpu.make_async_copy(labels_hbm, labels, sem)
    load_labels.start()
    out[...] = jnp.dot(feat[which], comp[which], preferred_element_type=F32)
    load_labels.wait()
    row = lax.broadcasted_iota(jnp.int32, (batch, batch), 0)
    col = lax.broadcasted_iota(jnp.int32, (batch, batch), 1)
    target[...] = jnp.sum(
        jnp.where(row == col, labels[...].astype(F32), 0.0), axis=1, keepdims=True
    )


def near(value):
    return pltpu.with_memory_space_constraint(value, pltpu.VMEM)


def far(value):
    return pltpu.with_memory_space_constraint(value, pltpu.HBM)


def terms(feat_t, compress, labels):
    _, batch, rows = feat_t.shape
    width = compress.shape[2]
    parts = 2
    cost = pl.CostEstimate(
        flops=2 * batch * rows * width, bytes_accessed=2 * rows * (width + batch), transcendentals=0
    )
    limit = pltpu.CompilerParams(vmem_limit_bytes=2 << 20)
    sent = pl.pallas_call(
        sent_kernel,
        out_shape=jax.ShapeDtypeStruct((batch, width), F32),
        in_specs=[ANY, ANY],
        out_specs=VMEM,
        scratch_shapes=[
            pltpu.VMEM((batch, rows), BF16),
            pltpu.VMEM((parts, rows // parts, width), BF16),
            pltpu.SemaphoreType.DMA((parts + 1,)),
        ],
        compiler_params=limit,
        cost_estimate=cost,
    )(far(feat_t), far(compress))
    kept, target = pl.pallas_call(
        kept_kernel,
        out_shape=(
            jax.ShapeDtypeStruct((batch, width), F32),
            jax.ShapeDtypeStruct((batch, 1), F32),
        ),
        in_specs=[VMEM, VMEM, ANY],
        out_specs=(VMEM, VMEM),
        scratch_shapes=[pltpu.VMEM((1, batch), labels.dtype), pltpu.SemaphoreType.DMA],
        compiler_params=limit,
        cost_estimate=cost,
    )(near(feat_t), near(compress), far(labels.reshape(1, batch)))
    return sent, kept, target


def products(pieces, down, upper, bias, wout, order):
    low = back = score = None
    width = pieces[0].shape[1]
    for piece, j in zip(pieces, order):
        rows = pl.ds(pl.multiple_of(j * width, width), width)
        scaled = piece.astype(F32) * wout[j]
        parts = (
            jnp.dot(piece, down[rows, :], preferred_element_type=F32),
            jnp.dot(scaled.astype(BF16), upper[rows, :], preferred_element_type=F32),
            scaled * (bias[j] + 1.0),
        )
        if low is None:
            low, back, score = parts
        else:
            low, back, score = low + parts[0], back + parts[1], score + parts[2]
    return low, back, score


def near_kernel(mine, down, upper, bias, wout, low, back, score):
    tower = lax.axis_index("tower")
    side = side_of(lax.axis_index("member"))
    low[...], back[...], score[...] = products(
        (mine[...],), down, upper, bias, wout, (2 * tower + side,)
    )


def top_kernel(
    mine, side_piece, tower_piece, both_piece, near_low, near_back, near_score,
    down, upper, bias, wout, target, feat, comp,
    grad_w_hbm, grad_x_hbm, grad_down_hbm, grad_up_hbm, vectors_hbm,
    compressed, gates, grad_w, grad_x, up_square, down_square, vectors, sems,
):
    tower, member = lax.axis_index("tower"), lax.axis_index("member")
    side = side_of(member)
    batch, width = mine.shape
    compressed[side] = mine[...]
    compressed[1 - side] = side_piece[...]
    other = 2 * (1 - tower)
    low_f, back, score = products(
        (side_piece[...], tower_piece[...], both_piece[...]),
        down,
        upper,
        bias,
        wout,
        (2 * tower + 1 - side, other + side, other + 1 - side),
    )
    low_f, back = near_low[...] + low_f, near_back[...] + back
    low, back_low = low_f.astype(BF16), back.astype(BF16)
    logit = jnp.sum(near_score[...] + score + low.astype(F32) * back, axis=1, keepdims=True)
    slopes = []
    for k in range(2):
        j = 2 * tower + k
        rows = pl.ds(pl.multiple_of(j * width, width), width)
        gate = nt(low, upper[rows, :]) + (bias[j] + 1.0)
        gates[k] = gate
        slopes.append(wout[j] * gate + nt(back_low, down[rows, :]))
    dlogit = 1.0 / (1.0 + jnp.exp(-logit)) - target[...]

    stores = []

    def send(source, target):
        stores.append(pltpu.make_async_copy(source, target, sems.at[len(stores)]))
        stores[-1].start()

    size = grad_w.shape[1]
    per_tower = CHUNKS // 2
    dcomps = [(dlogit * slope).astype(BF16) for slope in slopes]
    for i in range(CHUNKS):
        k, part = i // per_tower, i % per_tower
        grad_w[i] = contract_rows(feat[k, :, part * size : (part + 1) * size], dcomps[k])
        send(grad_w.at[i], grad_w_hbm.at[k, pl.ds(part * size, size)])
    for k in range(2):
        grad_x[k] = nt(dcomps[k], comp[k]).astype(BF16)
        send(grad_x.at[k], grad_x_hbm.at[k])

    count = grad_down_hbm.shape[0]
    first = (tower * lax.axis_size("member") + member) * count
    own = lax.div(first, width) - 2 * tower
    offset = pl.multiple_of(lax.rem(first, width), count)
    comp_f = compressed[own].astype(F32)
    dgate_f = dlogit * wout[2 * tower + own] * comp_f
    crossed = comp_f * gates[own]
    up_square[...] = contract_rows(dgate_f.astype(BF16), low)
    send(up_square.at[pl.ds(offset, count)], grad_up_hbm)
    down_square[...] = contract_rows(compressed[own], (dlogit * back).astype(BF16))
    send(down_square.at[pl.ds(offset, count)], grad_down_hbm)
    sums = jnp.concatenate(
        [
            jnp.sum(dgate_f, axis=0, keepdims=True),
            jnp.sum(dlogit * crossed, axis=0, keepdims=True),
            jnp.zeros((6, width), F32),
        ],
        axis=0,
    )
    vectors[...] = pltpu.roll(sums, width - offset, 1)[0:2, 0:count]
    send(vectors, vectors_hbm)
    for store in stores:
        store.wait()


def shards_doubling(features, compress, top_down, top_up, top_bias, out_weight, labels):
    local_towers, feat_rows, batch = features.shape
    width = compress.shape[2]
    rank = top_down.shape[1]
    members = lax.axis_size("member")
    top = top_down.shape[0]
    count = top // (2 * members)
    pieces = top // width
    feat_t = jnp.swapaxes(features, 1, 2)
    sent, kept, target = terms(feat_t, compress, labels)
    total = kept + exchange(sent, 0, 1)
    strides = [1 << bit for bit in range(1, members.bit_length() - 1)]
    if len(strides) > 1:
        one, two = strides.pop(0), strides.pop(0)
        total = total + sum(exchange(total, 0, bits) for bits in (one, two, one | two))
    for stride in strides:
        total = total + exchange(total.astype(BF16), 0, stride).astype(F32)
    mine = total.astype(BF16)
    side_piece = exchange(mine, 0, 1)
    tower_piece, both_piece = exchange(mine, 1, 0), exchange(mine, 1, 1)
    weights = (
        near(top_down),
        near(top_up),
        near(top_bias.reshape(pieces, 1, width)),
        near(out_weight.astype(F32).reshape(pieces, 1, width)),
    )
    near_sums = pl.pallas_call(
        near_kernel,
        out_shape=(jax.ShapeDtypeStruct((batch, rank), F32),) * 2
        + (jax.ShapeDtypeStruct((batch, width), F32),),
        in_specs=[VMEM] * 5,
        out_specs=(VMEM,) * 3,
        compiler_params=pltpu.CompilerParams(vmem_limit_bytes=4 << 20),
        cost_estimate=pl.CostEstimate(
            flops=4 * batch * width * rank, bytes_accessed=1 << 20, transcendentals=0
        ),
    )(near(mine), *weights)
    grad_w, grad_x, grad_down, grad_up, vectors = pl.pallas_call(
        top_kernel,
        out_shape=(
            jax.ShapeDtypeStruct((local_towers, feat_rows, width), F32),
            jax.ShapeDtypeStruct((local_towers, batch, feat_rows), BF16),
            jax.ShapeDtypeStruct((count, rank), F32),
            jax.ShapeDtypeStruct((count, rank), F32),
            jax.ShapeDtypeStruct((2, count), F32),
        ),
        in_specs=[VMEM] * 14,
        out_specs=(ANY,) * 5,
        scratch_shapes=[
            pltpu.VMEM((local_towers, batch, width), BF16),
            pltpu.VMEM((local_towers, batch, width), F32),
            pltpu.VMEM((CHUNKS, local_towers * feat_rows // CHUNKS, width), F32),
            pltpu.VMEM((local_towers, batch, feat_rows), BF16),
            pltpu.VMEM((width, rank), F32),
            pltpu.VMEM((width, rank), F32),
            pltpu.VMEM((2, count), F32),
            pltpu.SemaphoreType.DMA((CHUNKS + 5,)),
        ],
        compiler_params=pltpu.CompilerParams(vmem_limit_bytes=8 << 20),
        cost_estimate=pl.CostEstimate(
            flops=10 * batch * top * rank, bytes_accessed=4 << 20, transcendentals=batch
        ),
    )(
        near(mine),
        near(side_piece),
        near(tower_piece),
        near(both_piece),
        *(near(value) for value in near_sums),
        *weights,
        near(target),
        near(feat_t),
        near(compress),
    )
    return grad_w, jnp.swapaxes(grad_x, 1, 2), grad_down, grad_up, vectors


def shards(features, compress, top_down, *rest):
    towers, members = lax.axis_size("tower"), lax.axis_size("member")
    small = towers == 2 and features.shape[0] == 2 and features.shape[2] <= 128
    power = members > 1 and members & (members - 1) == 0
    body = shards_doubling if small and power else shards_spread
    return body(features, compress, top_down, *rest)


def solution(mesh):
    placed = (P("tower", "member", None), P("tower", "member", None), P(), P(), P(), P(), P())
    return jax.shard_map(
        shards,
        mesh=mesh,
        in_specs=placed,
        out_specs=(
            P("tower", "member", None),
            P("tower", "member", None),
            P(("tower", "member"), None),
            P(("tower", "member"), None),
            P(None, ("tower", "member")),
        ),
        check_vma=False,
    )
```
